256 devices in a mesh: dp: 32 (over x, y, core), mp: 8 (over z).
Axes of the slice: x: 4, y: 4, z: 8, core: 2. Of those that a mesh axis runs over, the one named last changes fastest.
Arguments:
- queries: bfloat16 [16384, 5120], P(('dp', 'mp')), may hold values from -22 to 22
- keys: bfloat16 [16384, 1024], P(('dp', 'mp')), may hold values from -6 to 6
- values: bfloat16 [16384, 1024], P(('dp', 'mp')), may hold values from -12 to 12
- prefix_keys: bfloat16 [32, 2048, 1024], P('dp', None, 'mp'), may hold values from -6 to 6
- prefix_values: bfloat16 [32, 2048, 1024], P('dp', None, 'mp'), may hold values from -12 to 12
- prompt_of: int32 [64], P('dp'), may hold values from 0 to 31, as said below
- lengths: int32 [64], P('dp'), may hold values from 32 to 256, as said below
- cotangent: bfloat16 [16384, 5120], P(('dp', 'mp')), may hold values from -20 to 20
Outputs:
- attended: bfloat16 [16384, 5120], P(('dp', 'mp'))
- d_queries: bfloat16 [16384, 5120], P(('dp', 'mp'))
- d_keys: bfloat16 [16384, 1024], P(('dp', 'mp'))
- d_values: bfloat16 [16384, 1024], P(('dp', 'mp'))
- d_prefix_keys: bfloat16 [32, 2048, 1024], P('dp', None, 'mp')
- d_prefix_values: bfloat16 [32, 2048, 1024], P('dp', None, 'mp')
The draws below stay inside these ranges and needn't reach their ends.
Inputs may be any that keep to these rules, and one draw needn't show every extreme that they name: `prompt_of`: prompt p is held at dp index p. The completions at dp index d (completions d * 2 to d * 2 + 1) belong to prompts max(d - 3, 0) to d; at some position r among them the completion belongs to prompt d - (d % 4), and the one at position (r + 1) % 2 belongs to prompt d. `lengths`: at least one completion has 256 live tokens.
All inputs are finite; a program needn't handle non-finite values.
Results may differ from the reference program's by a relative error of at most 0.012.
The reference program's roundings to bfloat16 on the way (of `weights`, `grad_out` and `d_scores`) count: a program that leaves them out, or rounds other values in their place, can miss the bound.
Values may be sent and summed in bfloat16 or wider, within the bound.
No kernel may reach another device: no remote copies, remote signals or barrier semaphores. Data moves between devices by JAX's collectives and lax.ppermute only.
A program may use at most 128 MiB of HBM per device.

```python
import jax
import jax.numpy as jnp
from jax import lax

QH = 40
KVH = 8
HD = 128
PREFIX = 2048
CLEN = 256
CMP_DEV = 2
REACH = 4
COMPL = 64
TOKENS = 16384
PROMPTS = 32
N_DP = 32


def draw_queries(key, part):
    key = jax.random.fold_in(key, 21)
    base = 1.5 * jnp.clip(jax.random.normal(key, (TOKENS, QH * HD), jnp.float32), -6.0, 6.0)
    return base.astype(jnp.bfloat16)


def draw_prefix_keys(key, part):
    key = jax.random.fold_in(key, 22)
    base = jnp.clip(jax.random.normal(key, (PROMPTS, PREFIX, KVH * HD), jnp.float32), -6.0, 6.0)
    return base.astype(jnp.bfloat16)


def draw_prompt_of(key, part):
    key = jax.random.fold_in(key, 23)
    offset_key = jax.random.fold_in(key, 1)
    place_key = jax.random.fold_in(key, 2)
    comp_ids = jnp.arange(COMPL, dtype=jnp.int32)
    device_ids = comp_ids // CMP_DEV
    position = comp_ids % CMP_DEV
    offsets = jax.random.randint(offset_key, (COMPL,), 0, REACH, jnp.int32)
    places = jax.random.randint(place_key, (N_DP,), 0, CMP_DEV, jnp.int32)
    chosen_place = jnp.sum(jnp.where(device_ids[:, None] == jnp.arange(N_DP, dtype=jnp.int32)[None, :], places[None, :], 0), 1).astype(jnp.int32)
    own_slot = position == (chosen_place + 1) % CMP_DEV
    offsets = jnp.where(own_slot, 0, offsets)
    forced = position == chosen_place
    offsets = jnp.where(forced, device_ids % REACH, offsets)
    return jnp.maximum(device_ids - offsets, 0).astype(jnp.int32)


def draw_lengths(key, part):
    key = jax.random.fold_in(key, 24)
    drawn = jax.random.randint(key, (COMPL,), max(CLEN // 8, 1), CLEN + 1, jnp.int32)
    return drawn.at[0].set(CLEN)


def block_levels(rng, dims, pieces, smallest, top_value):
    level, own = 1.0, jax.random.fold_in(rng, 6)
    for axis_at, parts in pieces:
        heights = jnp.exp(jax.random.uniform(jax.random.fold_in(own, axis_at), (parts,), jnp.float32, smallest / len(pieces), top_value / len(pieces)))
        level = level * jnp.repeat(heights, dims[axis_at] // parts).reshape([-1 if axis == axis_at else 1 for axis in range(len(dims))])
    return level


def scatter_about(stream_key, dims, deviation, limit, cuts=(), held_as=jnp.bfloat16):
    factor_of = block_levels(stream_key, dims, cuts, -0.22, 0.18) if cuts else 1.0
    values = jax.random.normal(stream_key, dims, jnp.float32) * deviation * factor_of
    return jnp.minimum(jnp.maximum(values, -limit), limit).astype(held_as)


def setup_inputs(seed: int = 0) -> dict:
    arg_keys = jax.random.split(jax.random.key(seed), 9)
    return {
        "queries": draw_queries(jax.random.fold_in(arg_keys[8], 71), 0),
        "keys": scatter_about(arg_keys[1], (TOKENS, KVH * HD), 1.0, 6.0, ((0, 256),)),
        "values": jnp.clip(jax.random.uniform(arg_keys[2], (TOKENS, KVH * HD), jnp.float32, -12.0, 12.0) * block_levels(arg_keys[2], (TOKENS, KVH * HD), ((0, 256),), -0.4, 0.0), -12.0, 12.0).astype(jnp.bfloat16),
        "prefix_keys": draw_prefix_keys(jax.random.fold_in(arg_keys[8], 71), 0),
        "prefix_values": jnp.clip(jax.random.uniform(arg_keys[4], (PROMPTS, PREFIX, KVH * HD), jnp.float32, -12.0, 12.0) * block_levels(arg_keys[4], (PROMPTS, PREFIX, KVH * HD), ((0, 32), (2, 8)), -0.4, 0.0), -12.0, 12.0).astype(jnp.bfloat16),
        "prompt_of": draw_prompt_of(jax.random.fold_in(arg_keys[8], 71), 0),
        "lengths": draw_lengths(jax.random.fold_in(arg_keys[8], 71), 0),
        "cotangent": jnp.clip(jax.random.uniform(arg_keys[7], (TOKENS, QH * HD), jnp.float32, -20.0, 20.0) * block_levels(arg_keys[7], (TOKENS, QH * HD), ((0, 256),), -0.4, 0.0), -20.0, 20.0).astype(jnp.bfloat16),
    }


masked_score = -1e30


def attend_one(query_rows, key_rows, value_rows, grad_rows, pre_keys, pre_values, length):
    clen = query_rows.shape[0]
    prefix = pre_keys.shape[0]
    head_dim = query_rows.shape[-1]
    scale = head_dim ** -0.5
    all_keys = jnp.concatenate([pre_keys, key_rows], 0).astype(jnp.float32)
    all_values = jnp.concatenate([pre_values, value_rows], 0).astype(jnp.float32)
    query_wide = query_rows.astype(jnp.float32)
    scores = jnp.einsum("tkgd,skd->kgts", query_wide, all_keys) * scale
    positions = jnp.arange(clen, dtype=jnp.int32)
    key_pos = jnp.arange(prefix + clen, dtype=jnp.int32) - prefix
    allowed = (key_pos[None, :] < 0) | ((key_pos[None, :] <= positions[:, None]) & (key_pos[None, :] < length))
    scores = jnp.where(allowed, scores, masked_score)
    top_score = jnp.max(scores, -1, keepdims=True)
    expo = jnp.exp(scores - top_score)
    probs = expo / jnp.sum(expo, -1, keepdims=True)
    weights = probs.astype(jnp.bfloat16).astype(jnp.float32)
    output = jnp.einsum("kgts,skd->tkgd", weights, all_values).astype(jnp.bfloat16)
    live_rows = (positions < length)[:, None, None, None]
    grad_out = jnp.where(live_rows, grad_rows, jnp.zeros((), grad_rows.dtype)).astype(jnp.float32)
    d_vals = jnp.einsum("kgts,tkgd->skd", weights, grad_out)
    d_probs = jnp.einsum("tkgd,skd->kgts", grad_out, all_values)
    delta = jnp.einsum("tkgd,tkgd->kgt", grad_out, output.astype(jnp.float32))
    d_scores = (probs * (d_probs - delta[..., None])).astype(jnp.bfloat16).astype(jnp.float32)
    d_query = (jnp.einsum("kgts,skd->tkgd", d_scores, all_keys) * scale).astype(jnp.bfloat16)
    d_keys_all = jnp.einsum("kgts,tkgd->skd", d_scores, query_wide) * scale
    return (output, d_query, d_keys_all[prefix:].astype(jnp.bfloat16), d_vals[prefix:].astype(jnp.bfloat16),
            d_keys_all[:prefix], d_vals[:prefix])


def reference(queries, keys, values, prefix_keys, prefix_values, prompt_of, lengths, cotangent):
    group_size = QH // KVH

    def per_completion(carry, index):
        grad_pk, grad_pv = carry
        start = (index * CLEN).astype(jnp.int32)
        query_rows = lax.dynamic_slice_in_dim(queries, start, CLEN, 0).reshape(CLEN, KVH, group_size, HD)
        grad_rows = lax.dynamic_slice_in_dim(cotangent, start, CLEN, 0).reshape(CLEN, KVH, group_size, HD)
        key_rows = lax.dynamic_slice_in_dim(keys, start, CLEN, 0).reshape(CLEN, KVH, HD)
        value_rows = lax.dynamic_slice_in_dim(values, start, CLEN, 0).reshape(CLEN, KVH, HD)
        prompt = prompt_of[index]
        pre_keys = prefix_keys[prompt].reshape(PREFIX, KVH, HD)
        pre_values = prefix_values[prompt].reshape(PREFIX, KVH, HD)
        output, d_query, d_key, d_value, d_pk, d_pv = attend_one(
            query_rows, key_rows, value_rows, grad_rows, pre_keys, pre_values, lengths[index])
        grad_pk = grad_pk.at[prompt].add(d_pk.reshape(PREFIX, KVH * HD))
        grad_pv = grad_pv.at[prompt].add(d_pv.reshape(PREFIX, KVH * HD))
        return (grad_pk, grad_pv), (output.reshape(CLEN, QH * HD), d_query.reshape(CLEN, QH * HD),
                                    d_key.reshape(CLEN, KVH * HD), d_value.reshape(CLEN, KVH * HD))

    zeros_acc = jnp.zeros((PROMPTS, PREFIX, KVH * HD), jnp.float32)
    (grad_pk, grad_pv), (output, d_query, d_key, d_value) = lax.scan(
        per_completion, (zeros_acc, zeros_acc), jnp.arange(COMPL, dtype=jnp.int32))
    return (output.reshape(TOKENS, QH * HD), d_query.reshape(TOKENS, QH * HD),
            d_key.reshape(TOKENS, KVH * HD), d_value.reshape(TOKENS, KVH * HD),
            grad_pk.astype(jnp.bfloat16), grad_pv.astype(jnp.bfloat16))
```

```python
import jax
import jax.numpy as jnp
from jax import lax
from jax.experimental import pallas as pl
from jax.experimental.pallas import tpu as pltpu
from jax.sharding import PartitionSpec as P

HD = 128
GROUP = 5
REACH = 4
CLEN = 256
PREFIX = 2048
CHUNK = 256
STEPS = PREFIX // CHUNK + 1
KEYS = PREFIX + CLEN
SCALE = HD**-0.5
SCALE_LOG2E = SCALE * 1.4426950408889634
MASKED = -1e30
HEADS_A = 2
HEADS_B = GROUP - HEADS_A
F32 = jnp.float32
BF16 = jnp.bfloat16


def nt(a, b):
    return lax.dot_general(a, b, (((1,), (1,)), ((), ())), preferred_element_type=F32)


def nn(a, b):
    return lax.dot_general(a, b, (((1,), (0,)), ((), ())), preferred_element_type=F32)


def pack_kernel(q_ref, k_ref, v_ref, g_ref, a_ref, b_ref):
    cut = HEADS_A * HD
    a_ref[0, :, :cut] = q_ref[:, :cut]
    a_ref[0, :, cut : 2 * cut] = g_ref[:, :cut]
    a_ref[0, :, 2 * cut : 2 * cut + HD] = k_ref[...]
    a_ref[0, :, 2 * cut + HD :] = v_ref[...]
    rest = HEADS_B * HD
    b_ref[0, :, :rest] = q_ref[:, cut:]
    b_ref[0, :, rest:] = g_ref[:, cut:]


def pack(queries, keys, values, cotangent, parts):
    rows = queries.shape[0]
    wide = pl.BlockSpec((rows, GROUP * HD), lambda m: (0, m))
    thin = pl.BlockSpec((rows, HD), lambda m: (0, m))
    wa, wb = (2 * HEADS_A + 2) * HD, 2 * HEADS_B * HD
    return pl.pallas_call(
        pack_kernel,
        grid=(parts,),
        in_specs=[wide, thin, thin, wide],
        out_specs=[
            pl.BlockSpec((1, rows, wa), lambda m: (m, 0, 0)),
            pl.BlockSpec((1, rows, wb), lambda m: (m, 0, 0)),
        ],
        out_shape=[
            jax.ShapeDtypeStruct((parts, rows, wa), BF16),
            jax.ShapeDtypeStruct((parts, rows, wb), BF16),
        ],
        name="pack",
    )(queries, keys, values, cotangent)


def unpack_kernel(a_ref, b_ref, o_ref, dq_ref, dk_ref, dv_ref):
    cut = HEADS_A * HD
    o_ref[:, :cut] = a_ref[0, :, :cut]
    dq_ref[:, :cut] = a_ref[0, :, cut:]
    rest = HEADS_B * HD
    o_ref[:, cut:] = b_ref[0, :, :rest]
    dq_ref[:, cut:] = b_ref[0, :, rest : 2 * rest]
    dk_ref[...] = b_ref[0, :, 2 * rest : 2 * rest + HD]
    dv_ref[...] = b_ref[0, :, 2 * rest + HD :]


def unpack(out_a, out_b):
    parts, rows, wa = out_a.shape
    wb = out_b.shape[2]
    wide = pl.BlockSpec((rows, GROUP * HD), lambda m: (0, m))
    thin = pl.BlockSpec((rows, HD), lambda m: (0, m))
    return pl.pallas_call(
        unpack_kernel,
        grid=(parts,),
        in_specs=[
            pl.BlockSpec((1, rows, wa), lambda m: (m, 0, 0)),
            pl.BlockSpec((1, rows, wb), lambda m: (m, 0, 0)),
        ],
        out_specs=[wide, wide, thin, thin],
        out_shape=[
            jax.ShapeDtypeStruct((rows, parts * GROUP * HD), BF16),
            jax.ShapeDtypeStruct((rows, parts * GROUP * HD), BF16),
            jax.ShapeDtypeStruct((rows, parts * HD), BF16),
            jax.ShapeDtypeStruct((rows, parts * HD), BF16),
        ],
        name="unpack",
    )(out_a, out_b)


def attend_kernel(heads, first, last, with_prev, *refs):
    slot_ref, len_ref, q_ref, g_ref, k_ref, v_ref, pk_ref, pv_ref = refs[:8]
    refs = refs[8:]
    if not first:
        acc_in_ref, refs = refs[0], refs[1:]
    if with_prev:
        refs = refs[1:]
    out_ref, acc_ref, s_ref, w_ref, kt_ref, vt_ref = refs
    j = pl.program_id(0)
    length = len_ref[slot_ref[0]]

    def key_rows(i):
        return k_ref[...] if i == STEPS - 1 else pk_ref[i * CHUNK : (i + 1) * CHUNK, :]

    def value_rows(i):
        return v_ref[...] if i == STEPS - 1 else pv_ref[i * CHUNK : (i + 1) * CHUNK, :]

    @pl.when(j == 0)
    def _():
        for i in range(STEPS):
            kt_ref[:, i * CHUNK : (i + 1) * CHUNK] = key_rows(i).T
            vt_ref[:, i * CHUNK : (i + 1) * CHUNK] = value_rows(i).T
        if first:
            acc_ref[...] = jnp.zeros_like(acc_ref)
        else:
            acc_ref[...] = acc_in_ref[...]

    q = q_ref[...]
    row = lax.broadcasted_iota(jnp.int32, (CLEN, HD), 0)
    g = jnp.where(row < length, g_ref[...], jnp.zeros((), BF16))
    gt = g.T
    top = jnp.full((1, CLEN), MASKED, F32)
    for i in range(STEPS):
        s = nt(key_rows(i), q)
        if i == STEPS - 1:
            kp = lax.broadcasted_iota(jnp.int32, (CHUNK, CLEN), 0)
            qp = lax.broadcasted_iota(jnp.int32, (CHUNK, CLEN), 1)
            s = jnp.where((kp <= qp) & (kp < length), s, MASKED)
        s_ref[i * CHUNK : (i + 1) * CHUNK, :] = s
        top = jnp.maximum(top, jnp.max(s, 0, keepdims=True))
    total = jnp.zeros((1, CLEN), F32)
    for i in range(STEPS):
        e = jnp.exp2((s_ref[i * CHUNK : (i + 1) * CHUNK, :] - top) * SCALE_LOG2E)
        total = total + jnp.sum(e, 0, keepdims=True)
        s_ref[i * CHUNK : (i + 1) * CHUNK, :] = e
    inv = 1.0 / total
    ot = jnp.zeros((HD, CLEN), F32)
    for i in range(STEPS):
        p = s_ref[i * CHUNK : (i + 1) * CHUNK, :] * inv
        w = p.astype(BF16)
        s_ref[i * CHUNK : (i + 1) * CHUNK, :] = p
        w_ref[i * CHUNK : (i + 1) * CHUNK, :] = w
        ot = ot + nn(vt_ref[:, i * CHUNK : (i + 1) * CHUNK], w)
    ob = ot.astype(BF16)
    out_ref[:, pl.ds(pl.multiple_of(j * HD, HD), HD)] = ob.T
    delta = jnp.sum(gt.astype(F32) * ob.astype(F32), 0, keepdims=True)
    dqt = jnp.zeros((HD, CLEN), F32)
    for i in range(STEPS):
        rows = slice(i * CHUNK, (i + 1) * CHUNK)
        dp = nt(value_rows(i), g)
        ds = (s_ref[rows, :] * (dp - delta)).astype(BF16)
        acc_ref[1, rows, :] += nn(w_ref[rows, :], g)
        acc_ref[0, rows, :] += nn(ds, q)
        dqt = dqt + nn(kt_ref[:, rows], ds)
    out_ref[:, pl.ds(pl.multiple_of((heads + j) * HD, HD), HD)] = (dqt * SCALE).astype(BF16).T
    if last:

        @pl.when(j == heads - 1)
        def _():
            acc_ref[0] = acc_ref[0] * SCALE
            out_ref[:, 2 * heads * HD : (2 * heads + 1) * HD] = acc_ref[0, PREFIX:, :].astype(BF16)
            out_ref[:, (2 * heads + 1) * HD :] = acc_ref[1, PREFIX:, :].astype(BF16)


def attend(heads, first, last, slot, lengths, rows_in, kv_rows, kv_col, prefix, acc, prev, name):
    rows = rows_in.shape[0]
    width = (2 * heads + (2 if last else 0)) * HD
    in_specs = [
        pl.BlockSpec((CLEN, HD), lambda j, s, n: (s[0], j)),
        pl.BlockSpec((CLEN, HD), lambda j, s, n: (s[0], heads + j)),
        pl.BlockSpec((CLEN, HD), lambda j, s, n: (s[0], kv_col)),
        pl.BlockSpec((CLEN, HD), lambda j, s, n: (s[0], kv_col + 1)),
        pl.BlockSpec((PREFIX, HD), lambda j, s, n: (0, 0)),
        pl.BlockSpec((PREFIX, HD), lambda j, s, n: (0, 0)),
    ]
    args = [rows_in, rows_in, kv_rows, kv_rows, *prefix]
    aliases = {}
    acc_spec = pl.BlockSpec((2, KEYS, HD), lambda j, s, n: (0, 0, 0))
    if not first:
        in_specs.append(acc_spec)
        args.append(acc)
    if prev is not None:
        aliases[2 + len(args)] = 0
        in_specs.append(pl.BlockSpec(memory_space=pl.ANY))
        args.append(prev)
    return pl.pallas_call(
        lambda *refs: attend_kernel(heads, first, last, prev is not None, *refs),
        grid_spec=pltpu.PrefetchScalarGridSpec(
            num_scalar_prefetch=2,
            grid=(heads,),
            in_specs=in_specs,
            out_specs=[pl.BlockSpec((CLEN, width), lambda j, s, n: (s[0], 0)), acc_spec],
            scratch_shapes=[
                pltpu.VMEM((KEYS, CLEN), F32),
                pltpu.VMEM((KEYS, CLEN), BF16),
                pltpu.VMEM((HD, KEYS), BF16),
                pltpu.VMEM((HD, KEYS), BF16),
            ],
        ),
        out_shape=[
            jax.ShapeDtypeStruct((rows, width), BF16),
            jax.ShapeDtypeStruct((2, KEYS, HD), F32),
        ],
        input_output_aliases=aliases,
        compiler_params=pltpu.CompilerParams(vmem_limit_bytes=40 * 1024 * 1024),
        cost_estimate=pl.CostEstimate(
            flops=heads * 12 * KEYS * CLEN * HD * 2, bytes_accessed=8 << 20, transcendentals=0
        ),
        name=name,
    )(slot, lengths, *args)


def exchange(rows, parts):
    out = lax.all_to_all(rows, "mp", split_axis=0, concat_axis=0, tiled=True)
    return out


def local(queries, keys, values, prefix_keys, prefix_values, prompt_of, lengths, cotangent):
    parts = lax.axis_size("mp")
    groups = lax.axis_size("dp") // REACH
    me = lax.axis_index("dp")
    leader = me % REACH == 0
    own = jnp.where(prompt_of[0] == me, 0, 1).astype(jnp.int32)
    own_slot = own[None]
    lead_slot = 1 - own_slot
    pk, pv = prefix_keys[0], prefix_values[0]

    def send(x, pairs):
        return lax.ppermute(
            x, "dp", [(REACH * n + a, REACH * n + b) for n in range(groups) for a, b in pairs]
        )

    far_k = send(pk, [(0, 2)])
    far_v = send(pv, [(0, 2)])
    base_k = jnp.where(leader, pk, far_k)
    base_v = jnp.where(leader, pv, far_v)
    near_k = send(base_k, [(0, 1), (2, 3)])
    near_v = send(base_v, [(0, 1), (2, 3)])
    odd = me % 2 == 1
    lead_k = jnp.where(odd, near_k, base_k)
    lead_v = jnp.where(odd, near_v, base_v)

    send_a, send_b = pack(queries, keys, values, cotangent, parts)
    rows_a = exchange(send_a, parts).reshape(-1, send_a.shape[2])
    rows_b = exchange(send_b, parts).reshape(-1, send_b.shape[2])
    kv = 2 * HEADS_A
    out_a, acc_own = attend(
        HEADS_A, True, False, own_slot, lengths, rows_a, rows_a, kv, (pk, pv), None, None, "own_a"
    )
    out_a, acc_lead = attend(
        HEADS_A, True, False, lead_slot, lengths, rows_a, rows_a, kv, (lead_k, lead_v), None, out_a, "lead_a"
    )
    out_b, acc_lead = attend(
        HEADS_B, False, True, lead_slot, lengths, rows_b, rows_a, kv, (lead_k, lead_v), acc_lead, None, "lead_b"
    )
    out_b, acc_own = attend(
        HEADS_B, False, True, own_slot, lengths, rows_b, rows_a, kv, (pk, pv), acc_own, out_b, "own_b"
    )
    rows = queries.shape[0]
    back_a = exchange(out_a.reshape(parts, rows, -1), parts)
    back_b = exchange(out_b.reshape(parts, rows, -1), parts)

    lead_grads = acc_lead[:, :PREFIX]
    near = send(lead_grads, [(1, 0), (3, 2)])
    pair_sum = lead_grads + near
    far = send(pair_sum, [(2, 0)])
    grads = acc_own[:, :PREFIX] + jnp.where(leader, pair_sum + far, 0.0)
    grads = grads.astype(BF16)
    attended, d_queries, d_keys, d_values = unpack(back_a, back_b)
    return (attended, d_queries, d_keys, d_values, grads[0][None], grads[1][None])


def solution(mesh):
    rows = P(("dp", "mp"), None)
    heads = P("dp", None, "mp")
    return jax.shard_map(
        local,
        mesh=mesh,
        in_specs=(rows, rows, rows, heads, heads, P("dp"), P("dp"), rows),
        out_specs=(rows, rows, rows, rows, heads, heads),
        check_vma=False,
    )
```

```python
import functools

import jax
import jax.numpy as jnp
from jax import lax
from jax.experimental import pallas as pl
from jax.experimental.pallas import tpu as pltpu
from jax.sharding import PartitionSpec as P

HD = 128
GROUP = 5
REACH = 4
CLEN = 256
PREFIX = 2048
CHUNK = 256
STEPS = PREFIX // CHUNK + 1
KEYS = PREFIX + CLEN
ROWS = 64
QUAD = 4
COLS = GROUP * CLEN
WIDE = GROUP * HD
PARTS = 8
SEND = 2 * WIDE + 2 * HD
SCALE = HD**-0.5
SCALE_LOG2E = SCALE * 1.4426950408889634
MASKED = -1e30
F32 = jnp.float32
BF16 = jnp.bfloat16
PIECE = PREFIX // 4
ANY = pl.BlockSpec(memory_space=pl.ANY)


def nt(a, b):
    return lax.dot_general(a, b, (((1,), (1,)), ((), ())), preferred_element_type=F32)


def nn(a, b):
    return lax.dot_general(a, b, (((1,), (0,)), ((), ())), preferred_element_type=F32)


def head_columns(part, width):
    return pl.ds(pl.multiple_of(part * width, HD), width)


def pack_kernel(q, k, v, g, pk, pv, prefix, out):
    prefix[0] = pk[...]
    prefix[1] = pv[...]
    for m in range(PARTS):
        wide, thin = slice(m * WIDE, (m + 1) * WIDE), slice(m * HD, (m + 1) * HD)
        out[m, :, :WIDE] = q[:, wide]
        out[m, :, WIDE : 2 * WIDE] = g[:, wide]
        out[m, :, 2 * WIDE : 2 * WIDE + HD] = k[:, thin]
        out[m, :, 2 * WIDE + HD :] = v[:, thin]


def pack(q, k, v, g, pk, pv):
    vmem = pl.BlockSpec(memory_space=pltpu.VMEM)
    return pl.pallas_call(
        pack_kernel,
        in_specs=[vmem] * 6,
        out_specs=[vmem] * 2,
        out_shape=[
            jax.ShapeDtypeStruct((2, PREFIX, HD), BF16),
            jax.ShapeDtypeStruct((PARTS, ROWS, SEND), BF16),
        ],
        name="pack",
    )(q, k, v, g, pk, pv)


def unpack_kernel(ids, *refs):
    bufs, (o, dq, dk, dv) = refs[:PARTS], refs[PARTS:]
    me = ids[1]
    for p in range(PARTS):
        cols = head_columns(me ^ p, WIDE)
        o[:, cols] = bufs[p][:, :WIDE]
        dq[:, cols] = bufs[p][:, WIDE : 2 * WIDE]
        cols = head_columns(me ^ p, HD)
        dk[:, cols] = bufs[p][:, 2 * WIDE : 2 * WIDE + HD]
        dv[:, cols] = bufs[p][:, 2 * WIDE + HD :]


def unpack(ids, bufs):
    vmem = pl.BlockSpec(memory_space=pltpu.VMEM)
    wide = jax.ShapeDtypeStruct((ROWS, PARTS * WIDE), BF16)
    thin = jax.ShapeDtypeStruct((ROWS, PARTS * HD), BF16)
    return pl.pallas_call(
        unpack_kernel,
        in_specs=[pl.BlockSpec(memory_space=pltpu.SMEM)] + [vmem] * PARTS,
        out_specs=[vmem] * 4,
        out_shape=[wide, wide, thin, thin],
        cost_estimate=pl.CostEstimate(flops=1 << 36, bytes_accessed=4 << 20, transcendentals=0),
        name="unpack",
    )(ids, *bufs)


def attend_kernel(far, chained, ids, prompt_of, lengths, *refs):
    bufs, refs = refs[0], refs[1:]
    pk, pv, far_prefix, near_prefix = refs[:4]
    refs = refs[4 + 2 * chained :]
    outs, refs = refs[:QUAD], refs[QUAD:]
    own_ref, lead_ref, q_ref, g_ref, k_own, v_own, e_ref, w_ref, d_ref = refs[:9]
    kt_ref, vt_ref, move_ref, pre_ref, acc_ref, pre_sem, acc_sem = refs[9:]
    dp_at, part = ids[0], ids[1]
    slot = (part >> 2) ^ far
    length = lengths[slot]
    role = jnp.where(slot == jnp.where(prompt_of[0] == dp_at, 0, 1), 0, 1)
    place = dp_at & 3
    source = jnp.where((role == 0) | (place == 0), 0, jnp.where(place == 2, 1, 2))
    places = [((part ^ n) & 3) * ROWS for n in range(QUAD)]

    def token_rows(n):
        return pl.ds(pl.multiple_of(places[n], ROWS), ROWS)

    sources = ((pk, pv), *((x.at[0], x.at[1]) for x in (far_prefix, near_prefix)))

    def prefix_copy(n, source_refs):
        return pltpu.make_async_copy(source_refs[n], pre_ref.at[n], pre_sem.at[n])

    for number, source_refs in enumerate(sources):

        @pl.when(source == number)
        def _(source_refs=source_refs):
            prefix_copy(0, source_refs).start()
            prefix_copy(1, source_refs).start()

    def key_rows(i):
        return k_own[...] if i == STEPS - 1 else pre_ref[0, rows[i], :]

    def value_rows(i):
        return v_own[...] if i == STEPS - 1 else pre_ref[1, rows[i], :]

    zero = jnp.zeros((), BF16)
    row = lax.broadcasted_iota(jnp.int32, (ROWS, HD), 0)
    for n in range(QUAD):
        live = n * ROWS + row < length
        k_own[n * ROWS : (n + 1) * ROWS, :] = bufs[n, :, 2 * WIDE : 2 * WIDE + HD]
        v_own[n * ROWS : (n + 1) * ROWS, :] = bufs[n, :, 2 * WIDE + HD :]
        for h in range(GROUP):
            at = slice(h * CLEN + n * ROWS, h * CLEN + (n + 1) * ROWS)
            q_ref[at, :] = bufs[n, :, h * HD : (h + 1) * HD]
            g_ref[at, :] = jnp.where(live, bufs[n, :, WIDE + h * HD : WIDE + (h + 1) * HD], zero)

    cols = [slice(h * CLEN, (h + 1) * CLEN) for h in range(GROUP)]
    rows = [slice(i * CHUNK, (i + 1) * CHUNK) for i in range(STEPS)]
    order = [STEPS - 1, *range(STEPS - 1)]
    tops, sums = [[] for _ in cols], [[] for _ in cols]
    scales, delta = [None] * GROUP, [None] * GROUP

    def scores(h, i):
        s = nt(key_rows(i), q_ref[cols[h], :])
        if i == STEPS - 1:
            key_at = lax.broadcasted_iota(jnp.int32, (CHUNK, CLEN), 0)
            query_at = lax.broadcasted_iota(jnp.int32, (CHUNK, CLEN), 1)
            s = jnp.where((key_at <= query_at) & (key_at < length), s, MASKED)
        top = jnp.max(s, 0, keepdims=True)
        e = jnp.exp2((s - top) * SCALE_LOG2E)
        e_ref[rows[i], cols[h]] = e
        tops[h].append(top)
        sums[h].append(jnp.sum(e, 0, keepdims=True))

    def normalise(h):
        best = functools.reduce(jnp.maximum, tops[h])
        parts = [jnp.exp2((t - best) * SCALE_LOG2E) for t in tops[h]]
        inv = 1.0 / functools.reduce(jnp.add, [f * s for f, s in zip(parts, sums[h])])
        scales[h] = {i: f * inv for i, f in zip(order, parts)}

    def give(column, x):
        move_ref[...] = x
        for n in range(QUAD):
            outs[n][:, column * HD : (column + 1) * HD] = move_ref[token_rows(n), :]

    def weigh(h, i):
        w_ref[rows[i], cols[h]] = (e_ref[rows[i], cols[h]] * scales[h][i]).astype(BF16)

    def attended(h):
        ob = nn(vt_ref[...], w_ref[:, cols[h]]).astype(BF16)
        gt = g_ref[cols[h], :].T
        delta[h] = jnp.sum(gt.astype(F32) * ob.astype(F32), 0, keepdims=True)
        give(h, ob.T)

    def d_scores(h, i):
        dp = nt(value_rows(i), g_ref[cols[h], :])
        probs = e_ref[rows[i], cols[h]] * scales[h][i]
        d_ref[rows[i], cols[h]] = (probs * (dp - delta[h])).astype(BF16)

    def d_queries(h):
        give(GROUP + h, (nn(kt_ref[...], d_ref[:, cols[h]]) * SCALE).astype(BF16).T)

    for n in range(GROUP + 2):
        for i in order:
            if n < 2 and i == 0:
                prefix_copy(n, sources[0]).wait()
            if n == 0:
                kt_ref[:, rows[i]] = key_rows(i).T
            if n == 1:
                vt_ref[:, rows[i]] = value_rows(i).T
            if n < GROUP:
                scores(n, i)
            if 1 <= n <= GROUP:
                weigh(n - 1, i)
            if n >= 2:
                d_scores(n - 2, i)
        if n < GROUP:
            normalise(n)
        if 1 <= n <= GROUP:
            attended(n - 1)
        if n >= 2:
            d_queries(n - 2)

    def store_copy(n, target):
        piece = pl.ds(n * PIECE, PIECE)
        return pltpu.make_async_copy(acc_ref.at[:, piece, :], target.at[:, piece, :], acc_sem.at[n])

    for i in order:
        dk = nn(d_ref[rows[i], :], q_ref[...]) * SCALE
        dv = nn(w_ref[rows[i], :], g_ref[...])
        if i == STEPS - 1:
            give(2 * GROUP, dk.astype(BF16))
            give(2 * GROUP + 1, dv.astype(BF16))
            continue
        acc_ref[0, rows[i], :] = dk
        acc_ref[1, rows[i], :] = dv
        if i % 2 == 1:

            @pl.when(role == 0)
            def _():
                store_copy(i // 2, own_ref).start()

            @pl.when(role == 1)
            def _():
                store_copy(i // 2, lead_ref).start()

    for n in range(4):
        store_copy(n, own_ref).wait()


def attend(name, far, scalars, rows, prefix, leads, chain=()):
    whole = pl.BlockSpec((ROWS, SEND), lambda n, *_: (0, 0))
    quad = pl.BlockSpec((QUAD, ROWS, SEND), lambda n, ids, *_: ((ids[1] >> 2) ^ far, 0, 0))
    args = [rows, *prefix, *leads, *chain]
    grads = jax.ShapeDtypeStruct((2, PREFIX, HD), F32)
    return pl.pallas_call(
        functools.partial(attend_kernel, far, len(chain) > 0),
        grid_spec=pltpu.PrefetchScalarGridSpec(
            num_scalar_prefetch=3,
            grid=(1,),
            in_specs=[quad] + [ANY] * (4 + len(chain)),
            out_specs=[whole] * QUAD + [ANY] * 2,
            scratch_shapes=[
                pltpu.VMEM((COLS, HD), BF16),
                pltpu.VMEM((COLS, HD), BF16),
                pltpu.VMEM((CLEN, HD), BF16),
                pltpu.VMEM((CLEN, HD), BF16),
                pltpu.VMEM((KEYS, COLS), F32),
                pltpu.VMEM((KEYS, COLS), BF16),
                pltpu.VMEM((KEYS, COLS), BF16),
                pltpu.VMEM((HD, KEYS), BF16),
                pltpu.VMEM((HD, KEYS), BF16),
                pltpu.VMEM((CLEN, HD), BF16),
                pltpu.VMEM((2, PREFIX, HD), BF16),
                pltpu.VMEM((2, PREFIX, HD), F32),
                pltpu.SemaphoreType.DMA((2,)),
                pltpu.SemaphoreType.DMA((4,)),
            ],
        ),
        out_shape=[jax.ShapeDtypeStruct((ROWS, SEND), BF16)] * QUAD + [grads] * 2,
        input_output_aliases={3 + len(args) - 2 + n: QUAD + n for n in range(len(chain))},
        compiler_params=pltpu.CompilerParams(vmem_limit_bytes=62 * 1024 * 1024),
        cost_estimate=pl.CostEstimate(flops=1 << 20, bytes_accessed=1 << 16, transcendentals=0),
        name=name,
    )(*scalars, *args)


def local(queries, keys, values, prefix_keys, prefix_values, prompt_of, lengths, cotangent):
    groups = lax.axis_size("dp") // REACH
    me, part = lax.axis_index("dp"), lax.axis_index("mp")
    pk, pv = prefix_keys[0], prefix_values[0]
    ids = jnp.stack([me, part]).astype(jnp.int32)
    scalars = (ids, prompt_of, lengths)

    def send(x, *pairs):
        return lax.ppermute(
            x, "dp", [(REACH * n + a, REACH * n + b) for n in range(groups) for a, b in pairs]
        )

    def swap(x, p):
        return lax.ppermute(x, "mp", [(i, i ^ p) for i in range(PARTS)])

    prefix, rows = pack(queries, keys, values, cotangent, pk, pv)
    leader = me % REACH == 0
    far = send(prefix, (0, 2))
    near = send(jnp.where(leader, prefix, far), (0, 1), (2, 3))
    leads = (far, near)
    rows = lax.all_to_all(rows, "mp", split_axis=0, concat_axis=0, tiled=True)
    *back_far, own_grads, lead_grads = attend("far", 1, scalars, rows, (pk, pv), leads)
    *back_near, own_grads, lead_grads = attend(
        "near", 0, scalars, rows, (pk, pv), leads, (own_grads, lead_grads)
    )
    back = back_near + back_far
    back = [back[0]] + [swap(back[p], p) for p in range(1, PARTS)]

    lead_grads, *back[4:6] = lax.optimization_barrier((lead_grads, *back[4:6]))
    near_sum = lead_grads + send(lead_grads, (1, 0), (3, 2))
    far_grads = send(near_sum.astype(BF16), (2, 0))
    base = own_grads + jnp.where(leader, near_sum, 0.0)
    d_keys, d_values = (
        (base[n] + far_grads[n].astype(F32)).astype(BF16)[None] for n in range(2)
    )
    outs = unpack(ids, back)
    return (*outs, d_keys, d_values)


def solution(mesh):
    rows = P(("dp", "mp"), None)
    heads = P("dp", None, "mp")
    return jax.shard_map(
        local,
        mesh=mesh,
        in_specs=(rows, rows, rows, heads, heads, P("dp"), P("dp"), rows),
        out_specs=(rows, rows, rows, rows, heads, heads),
        check_vma=False,
    )
```

```python
import functools

import jax
import jax.numpy as jnp
from jax import lax
from jax.experimental import pallas as pl
from jax.experimental.pallas import tpu as pltpu
from jax.sharding import PartitionSpec as P

HD = 128
GROUP = 5
REACH = 4
CLEN = 256
PREFIX = 2048
CHUNK = 256
STEPS = PREFIX // CHUNK + 1
KEYS = PREFIX + CLEN
ROWS = 64
QUAD = 4
COLS = GROUP * CLEN
WIDE = GROUP * HD
PARTS = 8
SEND = 2 * WIDE + 2 * HD
SCALE = HD**-0.5
SCALE_LOG2E = SCALE * 1.4426950408889634
MASKED = -1e30
F32 = jnp.float32
BF16 = jnp.bfloat16
PIECE = PREFIX // 4
ANY = pl.BlockSpec(memory_space=pl.ANY)


def nt(a, b):
    return lax.dot_general(a, b, (((1,), (1,)), ((), ())), preferred_element_type=F32)


def nn(a, b):
    return lax.dot_general(a, b, (((1,), (0,)), ((), ())), preferred_element_type=F32)


def head_columns(part, width):
    return pl.ds(pl.multiple_of(part * width, HD), width)


def pack_kernel(q, k, v, g, out):
    for m in range(PARTS):
        wide, thin = slice(m * WIDE, (m + 1) * WIDE), slice(m * HD, (m + 1) * HD)
        out[m, :, :WIDE] = q[:, wide]
        out[m, :, WIDE : 2 * WIDE] = g[:, wide]
        out[m, :, 2 * WIDE : 2 * WIDE + HD] = k[:, thin]
        out[m, :, 2 * WIDE + HD :] = v[:, thin]


def pack(q, k, v, g):
    vmem = pl.BlockSpec(memory_space=pltpu.VMEM)
    return pl.pallas_call(
        pack_kernel,
        in_specs=[vmem] * 4,
        out_specs=vmem,
        out_shape=jax.ShapeDtypeStruct((PARTS, ROWS, SEND), BF16),
        name="pack",
    )(q, k, v, g)


def unpack_kernel(ids, *refs):
    bufs, (near, _, o, dq, dk, dv) = refs[:QUAD], refs[QUAD:]
    me = ids[1]
    parts = [((me ^ QUAD) ^ p, bufs[p]) for p in range(QUAD)]
    parts += [((me & QUAD) + n, near.at[n]) for n in range(QUAD)]
    for m, part in parts:
        cols = head_columns(m, WIDE)
        o[:, cols] = part[:, :WIDE]
        dq[:, cols] = part[:, WIDE : 2 * WIDE]
        cols = head_columns(m, HD)
        dk[:, cols] = part[:, 2 * WIDE : 2 * WIDE + HD]
        dv[:, cols] = part[:, 2 * WIDE + HD :]


def unpack(ids, *bufs):
    vmem = pl.BlockSpec(memory_space=pltpu.VMEM)
    wide = jax.ShapeDtypeStruct((ROWS, PARTS * WIDE), BF16)
    thin = jax.ShapeDtypeStruct((ROWS, PARTS * HD), BF16)
    return pl.pallas_call(
        unpack_kernel,
        in_specs=[pl.BlockSpec(memory_space=pltpu.SMEM)] + [vmem] * (QUAD + 1) + [ANY],
        out_specs=[vmem] * 4,
        out_shape=[wide, wide, thin, thin],
        cost_estimate=pl.CostEstimate(flops=1 << 36, bytes_accessed=4 << 20, transcendentals=0),
        name="unpack",
    )(ids, *bufs)


def attend_kernel(far, chained, ids, prompt_of, lengths, *refs):
    rows_in, refs = refs[0], refs[1:]
    pk, pv, far_prefix, near_prefix = refs[:4]
    refs = refs[4 + 2 * chained :]
    sent = QUAD if far else 1
    outs, refs = refs[:sent], refs[sent:]
    own_ref, lead_ref, q_ref, g_ref, k_own, v_own, e_ref, w_ref, d_ref = refs[:9]
    kt_ref, vt_ref, move_ref, pre_ref, acc_ref, bufs, out_ref, pre_sem, acc_sem, row_sem, out_sem = refs[9:]
    dp_at, part = ids[0], ids[1]
    slot = (part >> 2) ^ far
    length = lengths[slot]
    role = jnp.where(slot == jnp.where(prompt_of[0] == dp_at, 0, 1), 0, 1)
    place = dp_at & 3
    source = jnp.where((role == 0) | (place == 0), 0, jnp.where(place == 2, 1, 2))
    places = [((part ^ n) & 3) * ROWS for n in range(QUAD)]
    rows_load = pltpu.make_async_copy(rows_in.at[pl.ds(slot * QUAD, QUAD)], bufs, row_sem)
    rows_load.start()

    def token_rows(n):
        return pl.ds(pl.multiple_of(places[n], ROWS), ROWS)

    sources = ((pk, pv), *((x.at[0], x.at[1]) for x in (far_prefix, near_prefix)))

    def prefix_copy(n, source_refs):
        return pltpu.make_async_copy(source_refs[n], pre_ref.at[n], pre_sem.at[n])

    for number, source_refs in enumerate(sources):

        @pl.when(source == number)
        def _(source_refs=source_refs):
            prefix_copy(0, source_refs).start()
            prefix_copy(1, source_refs).start()

    def key_rows(i):
        return k_own[...] if i == STEPS - 1 else pre_ref[0, rows[i], :]

    def value_rows(i):
        return v_own[...] if i == STEPS - 1 else pre_ref[1, rows[i], :]

    rows_load.wait()
    zero = jnp.zeros((), BF16)
    row = lax.broadcasted_iota(jnp.int32, (ROWS, HD), 0)
    for n in range(QUAD):
        live = n * ROWS + row < length
        k_own[n * ROWS : (n + 1) * ROWS, :] = bufs[n, :, 2 * WIDE : 2 * WIDE + HD]
        v_own[n * ROWS : (n + 1) * ROWS, :] = bufs[n, :, 2 * WIDE + HD :]
        for h in range(GROUP):
            at = slice(h * CLEN + n * ROWS, h * CLEN + (n + 1) * ROWS)
            q_ref[at, :] = bufs[n, :, h * HD : (h + 1) * HD]
            g_ref[at, :] = jnp.where(live, bufs[n, :, WIDE + h * HD : WIDE + (h + 1) * HD], zero)

    cols = [slice(h * CLEN, (h + 1) * CLEN) for h in range(GROUP)]
    rows = [slice(i * CHUNK, (i + 1) * CHUNK) for i in range(STEPS)]
    order = [STEPS - 1, *range(STEPS - 1)]
    tops, sums = [[] for _ in cols], [[] for _ in cols]
    scales, delta = [None] * GROUP, [None] * GROUP

    def scores(h, i):
        s = nt(key_rows(i), q_ref[cols[h], :])
        if i == STEPS - 1:
            key_at = lax.broadcasted_iota(jnp.int32, (CHUNK, CLEN), 0)
            query_at = lax.broadcasted_iota(jnp.int32, (CHUNK, CLEN), 1)
            s = jnp.where((key_at <= query_at) & (key_at < length), s, MASKED)
        top = jnp.max(s, 0, keepdims=True)
        e = jnp.exp2((s - top) * SCALE_LOG2E)
        e_ref[rows[i], cols[h]] = e
        tops[h].append(top)
        sums[h].append(jnp.sum(e, 0, keepdims=True))

    def normalise(h):
        best = functools.reduce(jnp.maximum, tops[h])
        parts = [jnp.exp2((t - best) * SCALE_LOG2E) for t in tops[h]]
        inv = 1.0 / functools.reduce(jnp.add, [f * s for f, s in zip(parts, sums[h])])
        scales[h] = {i: f * inv for i, f in zip(order, parts)}

    def give(column, x):
        move_ref[...] = x
        for n in range(QUAD):
            at = token_rows(n) if far else pl.ds(n * ROWS, ROWS)
            out_ref[n, :, column * HD : (column + 1) * HD] = move_ref[at, :]

    def weigh(h, i):
        w_ref[rows[i], cols[h]] = (e_ref[rows[i], cols[h]] * scales[h][i]).astype(BF16)

    def attended(h):
        ob = nn(vt_ref[...], w_ref[:, cols[h]]).astype(BF16)
        gt = g_ref[cols[h], :].T
        delta[h] = jnp.sum(gt.astype(F32) * ob.astype(F32), 0, keepdims=True)
        give(h, ob.T)

    def d_scores(h, i):
        dp = nt(value_rows(i), g_ref[cols[h], :])
        probs = e_ref[rows[i], cols[h]] * scales[h][i]
        d_ref[rows[i], cols[h]] = (probs * (dp - delta[h])).astype(BF16)

    def d_queries(h):
        give(GROUP + h, (nn(kt_ref[...], d_ref[:, cols[h]]) * SCALE).astype(BF16).T)

    early = slice(0, (GROUP - 2) * CLEN)
    late = slice((GROUP - 2) * CLEN, COLS)

    def sums_over(i, of):
        dk = nn(d_ref[rows[i], of], q_ref[of, :])
        dv = nn(w_ref[rows[i], of], g_ref[of, :])
        return dk, dv

    def early_sums(i):
        acc_ref[0, rows[i], :], acc_ref[1, rows[i], :] = sums_over(i, early)

    for n in range(GROUP + 2):
        for i in order:
            if n < 2 and i == 0:
                prefix_copy(n, sources[0]).wait()
            if n == 0:
                kt_ref[:, rows[i]] = key_rows(i).T
            if n == 1:
                vt_ref[:, rows[i]] = value_rows(i).T
            if n < GROUP:
                scores(n, i)
            if 1 <= n <= GROUP:
                weigh(n - 1, i)
            if n >= 2:
                d_scores(n - 2, i)
            if n == GROUP:
                early_sums(i)
        if n < GROUP:
            normalise(n)
        if 1 <= n <= GROUP:
            attended(n - 1)
        if n >= 2:
            d_queries(n - 2)

    def store_copy(n, target):
        piece = pl.ds(n * PIECE, PIECE)
        return pltpu.make_async_copy(acc_ref.at[:, piece, :], target.at[:, piece, :], acc_sem.at[n])

    pieces = [out_ref.at[n] for n in range(QUAD)] if far else [out_ref]
    results = [
        pltpu.make_async_copy(pieces[n], outs[n], out_sem.at[n]) for n in range(sent)
    ]
    for i in order:
        dk, dv = sums_over(i, late)
        dk = (acc_ref[0, rows[i], :] + dk) * SCALE
        dv = acc_ref[1, rows[i], :] + dv
        if i == STEPS - 1:
            give(2 * GROUP, dk.astype(BF16))
            give(2 * GROUP + 1, dv.astype(BF16))
            for copy in results:
                copy.start()
            continue
        acc_ref[0, rows[i], :] = dk
        acc_ref[1, rows[i], :] = dv
        if i % 2 == 1:

            @pl.when(role == 0)
            def _():
                store_copy(i // 2, own_ref).start()

            @pl.when(role == 1)
            def _():
                store_copy(i // 2, lead_ref).start()

    for copy in results:
        copy.wait()
    for n in range(4):
        store_copy(n, own_ref).wait()


def attend(name, far, scalars, rows, prefix, leads, chain=()):
    args = [rows, *prefix, *leads, *chain]
    sent = [(ROWS, SEND)] * QUAD if far else [(QUAD, ROWS, SEND)]
    grads = jax.ShapeDtypeStruct((2, PREFIX, HD), F32)
    return pl.pallas_call(
        functools.partial(attend_kernel, far, len(chain) > 0),
        grid_spec=pltpu.PrefetchScalarGridSpec(
            num_scalar_prefetch=3,
            grid=(1,),
            in_specs=[ANY] * (5 + len(chain)),
            out_specs=[ANY] * (len(sent) + 2),
            scratch_shapes=[
                pltpu.VMEM((COLS, HD), BF16),
                pltpu.VMEM((COLS, HD), BF16),
                pltpu.VMEM((CLEN, HD), BF16),
                pltpu.VMEM((CLEN, HD), BF16),
                pltpu.VMEM((KEYS, COLS), F32),
                pltpu.VMEM((KEYS, COLS), BF16),
                pltpu.VMEM((KEYS, COLS), BF16),
                pltpu.VMEM((HD, KEYS), BF16),
                pltpu.VMEM((HD, KEYS), BF16),
                pltpu.VMEM((CLEN, HD), BF16),
                pltpu.VMEM((2, PREFIX, HD), BF16),
                pltpu.VMEM((2, KEYS, HD), F32),
                pltpu.VMEM((QUAD, ROWS, SEND), BF16),
                pltpu.VMEM((QUAD, ROWS, SEND), BF16),
                pltpu.SemaphoreType.DMA((2,)),
                pltpu.SemaphoreType.DMA((4,)),
                pltpu.SemaphoreType.DMA(()),
                pltpu.SemaphoreType.DMA((QUAD,)),
            ],
        ),
        out_shape=[jax.ShapeDtypeStruct(x, BF16) for x in sent] + [grads] * 2,
        input_output_aliases={3 + len(args) - 2 + n: len(sent) + n for n in range(len(chain))},
        compiler_params=pltpu.CompilerParams(vmem_limit_bytes=63 * 1024 * 1024),
        cost_estimate=pl.CostEstimate(flops=1 << 20, bytes_accessed=1 << 16, transcendentals=0),
        name=name,
    )(*scalars, *args)


def local(queries, keys, values, prefix_keys, prefix_values, prompt_of, lengths, cotangent):
    groups = lax.axis_size("dp") // REACH
    me, part = lax.axis_index("dp"), lax.axis_index("mp")
    pk, pv = prefix_keys[0], prefix_values[0]
    ids = jnp.stack([me, part]).astype(jnp.int32)
    scalars = (ids, prompt_of, lengths)

    def send(x, *pairs):
        return lax.ppermute(
            x, "dp", [(REACH * n + a, REACH * n + b) for n in range(groups) for a, b in pairs]
        )

    def swap(x, p):
        return lax.ppermute(x, "mp", [(i, i ^ p) for i in range(PARTS)])

    rows = pack(queries, keys, values, cotangent)
    rows, *prefix = lax.optimization_barrier((rows, prefix_keys, prefix_values))
    prefix = jnp.concatenate(prefix, 0)
    leader = me % REACH == 0
    far = send(prefix, (0, 2))
    near = send(jnp.where(leader, prefix, far), (0, 1), (2, 3))
    leads = (far, near)
    rows = lax.all_to_all(rows, "mp", split_axis=0, concat_axis=0, tiled=True)
    *back, own_grads, lead_grads = attend("far", 1, scalars, rows, (pk, pv), leads)
    back_near, own_grads, lead_grads = attend(
        "near", 0, scalars, rows, (pk, pv), leads, (own_grads, lead_grads)
    )
    back = [swap(x, QUAD + n) for n, x in enumerate(back)]
    quads = [list(range(n, n + QUAD)) for n in range(0, PARTS, QUAD)]
    back_near = lax.all_to_all(
        back_near, "mp", split_axis=0, concat_axis=0, axis_index_groups=quads, tiled=True
    )

    lead_grads, *back[:2] = lax.optimization_barrier((lead_grads, *back[:2]))
    near_grads = send(lead_grads, (1, 0), (3, 2))
    near_sum = (lead_grads + near_grads).astype(BF16)
    far_grads = send(near_sum, (2, 0))
    near_sum, near_grads = lax.optimization_barrier((near_sum, near_grads))
    base = own_grads + jnp.where(leader, lead_grads + near_grads, 0.0)
    d_keys, d_values = (
        (base[n] + far_grads[n].astype(F32)).astype(BF16)[None] for n in range(2)
    )
    outs = unpack(ids, *back, back_near, base)
    return (*outs, d_keys, d_values)


def solution(mesh):
    rows = P(("dp", "mp"), None)
    heads = P("dp", None, "mp")
    return jax.shard_map(
        local,
        mesh=mesh,
        in_specs=(rows, rows, rows, heads, heads, P("dp"), P("dp"), rows),
        out_specs=(rows, rows, rows, rows, heads, heads),
        check_vma=False,
    )
```

```python
import functools

import jax
import jax.numpy as jnp
from jax import lax
from jax.experimental import pallas as pl
from jax.experimental.pallas import tpu as pltpu
from jax.sharding import PartitionSpec as P

HD = 128
GROUP = 5
REACH = 4
CLEN = 256
PREFIX = 2048
CHUNK = 256
STEPS = PREFIX // CHUNK + 1
KEYS = PREFIX + CLEN
ROWS = 64
QUAD = 4
COLS = GROUP * CLEN
WIDE = GROUP * HD
PARTS = 8
SEND = 2 * WIDE + 2 * HD
SCALE = HD**-0.5
SCALE_LOG2E = SCALE * 1.4426950408889634
MASKED = -1e30
F32 = jnp.float32
BF16 = jnp.bfloat16
PIECE = PREFIX // 4
ANY = pl.BlockSpec(memory_space=pl.ANY)


def nt(a, b):
    return lax.dot_general(a, b, (((1,), (1,)), ((), ())), preferred_element_type=F32)


def nn(a, b):
    return lax.dot_general(a, b, (((1,), (0,)), ((), ())), preferred_element_type=F32)


def head_columns(part, width):
    return pl.ds(pl.multiple_of(part * width, HD), width)


def pack_kernel(q, k, v, g, out):
    for m in range(QUAD):
        wide, thin = slice(m * WIDE, (m + 1) * WIDE), slice(m * HD, (m + 1) * HD)
        out[m, :, :WIDE] = q[:, wide]
        out[m, :, WIDE : 2 * WIDE] = g[:, wide]
        out[m, :, 2 * WIDE : 2 * WIDE + HD] = k[:, thin]
        out[m, :, 2 * WIDE + HD :] = v[:, thin]


def pack(q, k, v, g):
    wide = pl.BlockSpec((ROWS, QUAD * WIDE), lambda n: (0, n))
    thin = pl.BlockSpec((ROWS, QUAD * HD), lambda n: (0, n))
    return pl.pallas_call(
        pack_kernel,
        grid=(PARTS // QUAD,),
        in_specs=[wide, thin, thin, wide],
        out_specs=pl.BlockSpec((QUAD, ROWS, SEND), lambda n: (n, 0, 0)),
        out_shape=jax.ShapeDtypeStruct((PARTS, ROWS, SEND), BF16),
        name="pack",
    )(q, k, v, g)


def unpack_kernel(ids, *refs):
    bufs, (near, _, o, dq, dk, dv) = refs[:QUAD], refs[QUAD:]
    me = ids[1]
    parts = [((me ^ QUAD) ^ p, bufs[p]) for p in range(QUAD)]
    parts += [((me & QUAD) + n, near.at[n]) for n in range(QUAD)]
    for m, part in parts:
        cols = head_columns(m, WIDE)
        o[:, cols] = part[:, :WIDE]
        dq[:, cols] = part[:, WIDE : 2 * WIDE]
        cols = head_columns(m, HD)
        dk[:, cols] = part[:, 2 * WIDE : 2 * WIDE + HD]
        dv[:, cols] = part[:, 2 * WIDE + HD :]


def unpack(ids, *bufs):
    vmem = pl.BlockSpec(memory_space=pltpu.VMEM)
    wide = jax.ShapeDtypeStruct((ROWS, PARTS * WIDE), BF16)
    thin = jax.ShapeDtypeStruct((ROWS, PARTS * HD), BF16)
    return pl.pallas_call(
        unpack_kernel,
        in_specs=[pl.BlockSpec(memory_space=pltpu.SMEM)] + [vmem] * (QUAD + 1) + [ANY],
        out_specs=[vmem] * 4,
        out_shape=[wide, wide, thin, thin],
        cost_estimate=pl.CostEstimate(flops=1 << 36, bytes_accessed=4 << 20, transcendentals=0),
        name="unpack",
    )(ids, *bufs)


def attend_kernel(far, chained, ids, prompt_of, lengths, *refs):
    rows_in, refs = refs[0], refs[1:]
    pk, pv, far_prefix, near_prefix = refs[:4]
    refs = refs[4 + 2 * chained :]
    sent = QUAD if far else 1
    outs, refs = refs[:sent], refs[sent:]
    own_ref, lead_ref, q_ref, g_ref, k_own, v_own, e_ref, w_ref, d_ref = refs[:9]
    kt_ref, vt_ref, move_ref, pre_ref, acc_ref, bufs, out_ref, pre_sem, acc_sem, row_sem, out_sem = refs[9:]
    dp_at, part = ids[0], ids[1]
    slot = (part >> 2) ^ far
    length = lengths[slot]
    role = jnp.where(slot == jnp.where(prompt_of[0] == dp_at, 0, 1), 0, 1)
    place = dp_at & 3
    source = jnp.where((role == 0) | (place == 0), 0, jnp.where(place == 2, 1, 2))
    places = [((part ^ n) & 3) * ROWS for n in range(QUAD)]
    rows_load = pltpu.make_async_copy(rows_in.at[pl.ds(slot * QUAD, QUAD)], bufs, row_sem)
    rows_load.start()

    def token_rows(n):
        return pl.ds(pl.multiple_of(places[n], ROWS), ROWS)

    sources = ((pk, pv), *((x.at[0], x.at[1]) for x in (far_prefix, near_prefix)))

    def prefix_copy(n, source_refs):
        return pltpu.make_async_copy(source_refs[n], pre_ref.at[n], pre_sem.at[n])

    for number, source_refs in enumerate(sources):

        @pl.when(source == number)
        def _(source_refs=source_refs):
            prefix_copy(0, source_refs).start()
            prefix_copy(1, source_refs).start()

    def key_rows(i):
        return k_own[...] if i == STEPS - 1 else pre_ref[0, rows[i], :]

    def value_rows(i):
        return v_own[...] if i == STEPS - 1 else pre_ref[1, rows[i], :]

    rows_load.wait()
    zero = jnp.zeros((), BF16)
    row = lax.broadcasted_iota(jnp.int32, (ROWS, HD), 0)
    for n in range(QUAD):
        live = n * ROWS + row < length
        k_own[n * ROWS : (n + 1) * ROWS, :] = bufs[n, :, 2 * WIDE : 2 * WIDE + HD]
        v_own[n * ROWS : (n + 1) * ROWS, :] = bufs[n, :, 2 * WIDE + HD :]
        for h in range(GROUP):
            at = slice(h * CLEN + n * ROWS, h * CLEN + (n + 1) * ROWS)
            q_ref[at, :] = bufs[n, :, h * HD : (h + 1) * HD]
            g_ref[at, :] = jnp.where(live, bufs[n, :, WIDE + h * HD : WIDE + (h + 1) * HD], zero)

    cols = [slice(h * CLEN, (h + 1) * CLEN) for h in range(GROUP)]
    rows = [slice(i * CHUNK, (i + 1) * CHUNK) for i in range(STEPS)]
    order = [STEPS - 1, *range(STEPS - 1)]
    tops, sums = [[] for _ in cols], [[] for _ in cols]
    scales, delta = [None] * GROUP, [None] * GROUP

    def scores(h, i):
        s = nt(key_rows(i), q_ref[cols[h], :])
        if i == STEPS - 1:
            key_at = lax.broadcasted_iota(jnp.int32, (CHUNK, CLEN), 0)
            query_at = lax.broadcasted_iota(jnp.int32, (CHUNK, CLEN), 1)
            s = jnp.where((key_at <= query_at) & (key_at < length), s, MASKED)
        top = jnp.max(s, 0, keepdims=True)
        e = jnp.exp2((s - top) * SCALE_LOG2E)
        e_ref[rows[i], cols[h]] = e
        tops[h].append(top)
        sums[h].append(jnp.sum(e, 0, keepdims=True))

    def normalise(h):
        best = functools.reduce(jnp.maximum, tops[h])
        parts = [jnp.exp2((t - best) * SCALE_LOG2E) for t in tops[h]]
        inv = 1.0 / functools.reduce(jnp.add, [f * s for f, s in zip(parts, sums[h])])
        scales[h] = {i: f * inv for i, f in zip(order, parts)}

    def give(column, x):
        move_ref[...] = x
        for n in range(QUAD):
            at = token_rows(n) if far else pl.ds(n * ROWS, ROWS)
            out_ref[n, :, column * HD : (column + 1) * HD] = move_ref[at, :]

    def weigh(h, i):
        w_ref[rows[i], cols[h]] = (e_ref[rows[i], cols[h]] * scales[h][i]).astype(BF16)

    def attended(h):
        ob = nn(vt_ref[...], w_ref[:, cols[h]]).astype(BF16)
        gt = g_ref[cols[h], :].T
        delta[h] = jnp.sum(gt.astype(F32) * ob.astype(F32), 0, keepdims=True)
        give(h, ob.T)

    def d_scores(h, i):
        dp = nt(value_rows(i), g_ref[cols[h], :])
        probs = e_ref[rows[i], cols[h]] * scales[h][i]
        d_ref[rows[i], cols[h]] = (probs * (dp - delta[h])).astype(BF16)

    def d_queries(h):
        give(GROUP + h, (nn(kt_ref[...], d_ref[:, cols[h]]) * SCALE).astype(BF16).T)

    early = slice(0, (GROUP - 2) * CLEN)
    late = slice((GROUP - 2) * CLEN, COLS)

    def sums_over(i, of):
        dk = nn(d_ref[rows[i], of], q_ref[of, :])
        dv = nn(w_ref[rows[i], of], g_ref[of, :])
        return dk, dv

    def early_sums(i):
        acc_ref[0, rows[i], :], acc_ref[1, rows[i], :] = sums_over(i, early)

    for n in range(GROUP + 2):
        for i in order:
            if n < 2 and i == 0:
                prefix_copy(n, sources[0]).wait()
            if n == 0:
                kt_ref[:, rows[i]] = key_rows(i).T
            if n == 1:
                vt_ref[:, rows[i]] = value_rows(i).T
            if n < GROUP:
                scores(n, i)
            if 1 <= n <= GROUP:
                weigh(n - 1, i)
            if n >= 2:
                d_scores(n - 2, i)
            if n == GROUP:
                early_sums(i)
        if n < GROUP:
            normalise(n)
        if 1 <= n <= GROUP:
            attended(n - 1)
        if n >= 2:
            d_queries(n - 2)

    def store_copy(n, target):
        piece = pl.ds(n * PIECE, PIECE)
        return pltpu.make_async_copy(acc_ref.at[:, piece, :], target.at[:, piece, :], acc_sem.at[n])

    pieces = [out_ref.at[n] for n in range(QUAD)] if far else [out_ref]
    results = [
        pltpu.make_async_copy(pieces[n], outs[n], out_sem.at[n]) for n in range(sent)
    ]
    for i in order:
        dk, dv = sums_over(i, late)
        dk = (acc_ref[0, rows[i], :] + dk) * SCALE
        dv = acc_ref[1, rows[i], :] + dv
        if i == STEPS - 1:
            give(2 * GROUP, dk.astype(BF16))
            give(2 * GROUP + 1, dv.astype(BF16))
            for copy in results:
                copy.start()
            continue
        acc_ref[0, rows[i], :] = dk
        acc_ref[1, rows[i], :] = dv
        if i % 2 == 1:

            @pl.when(role == 0)
            def _():
                store_copy(i // 2, own_ref).start()

            @pl.when(role == 1)
            def _():
                store_copy(i // 2, lead_ref).start()

    for copy in results:
        copy.wait()
    for n in range(4):
        store_copy(n, own_ref).wait()


def attend(name, far, scalars, rows, prefix, leads, chain=()):
    args = [rows, *prefix, *leads, *chain]
    sent = [(ROWS, SEND)] * QUAD if far else [(QUAD, ROWS, SEND)]
    grads = jax.ShapeDtypeStruct((2, PREFIX, HD), F32)
    return pl.pallas_call(
        functools.partial(attend_kernel, far, len(chain) > 0),
        grid_spec=pltpu.PrefetchScalarGridSpec(
            num_scalar_prefetch=3,
            grid=(1,),
            in_specs=[ANY] * (5 + len(chain)),
            out_specs=[ANY] * (len(sent) + 2),
            scratch_shapes=[
                pltpu.VMEM((COLS, HD), BF16),
                pltpu.VMEM((COLS, HD), BF16),
                pltpu.VMEM((CLEN, HD), BF16),
                pltpu.VMEM((CLEN, HD), BF16),
                pltpu.VMEM((KEYS, COLS), F32),
                pltpu.VMEM((KEYS, COLS), BF16),
                pltpu.VMEM((KEYS, COLS), BF16),
                pltpu.VMEM((HD, KEYS), BF16),
                pltpu.VMEM((HD, KEYS), BF16),
                pltpu.VMEM((CLEN, HD), BF16),
                pltpu.VMEM((2, PREFIX, HD), BF16),
                pltpu.VMEM((2, KEYS, HD), F32),
                pltpu.VMEM((QUAD, ROWS, SEND), BF16),
                pltpu.VMEM((QUAD, ROWS, SEND), BF16),
                pltpu.SemaphoreType.DMA((2,)),
                pltpu.SemaphoreType.DMA((4,)),
                pltpu.SemaphoreType.DMA(()),
                pltpu.SemaphoreType.DMA((QUAD,)),
            ],
        ),
        out_shape=[jax.ShapeDtypeStruct(x, BF16) for x in sent] + [grads] * 2,
        input_output_aliases={3 + len(args) - 2 + n: len(sent) + n for n in range(len(chain))},
        compiler_params=pltpu.CompilerParams(vmem_limit_bytes=63 * 1024 * 1024),
        cost_estimate=pl.CostEstimate(flops=1 << 20, bytes_accessed=1 << 16, transcendentals=0),
        name=name,
    )(*scalars, *args)


def local(queries, keys, values, prefix_keys, prefix_values, prompt_of, lengths, cotangent):
    groups = lax.axis_size("dp") // REACH
    me, part = lax.axis_index("dp"), lax.axis_index("mp")
    pk, pv = prefix_keys[0], prefix_values[0]
    ids = jnp.stack([me, part]).astype(jnp.int32)
    scalars = (ids, prompt_of, lengths)

    def send(x, *pairs):
        return lax.ppermute(
            x, "dp", [(REACH * n + a, REACH * n + b) for n in range(groups) for a, b in pairs]
        )

    def swap(x, p):
        return lax.ppermute(x, "mp", [(i, i ^ p) for i in range(PARTS)])

    rows = pack(queries, keys, values, cotangent)
    rows, *prefix = lax.optimization_barrier((rows, prefix_keys, prefix_values))
    prefix = jnp.concatenate(prefix, 0)
    leader = me % REACH == 0
    far = send(prefix, (0, 2))
    near = send(jnp.where(leader, prefix, far), (0, 1), (2, 3))
    leads = (far, near)
    rows = lax.all_to_all(rows, "mp", split_axis=0, concat_axis=0, tiled=True)
    *back, own_grads, lead_grads = attend("far", 1, scalars, rows, (pk, pv), leads)
    back_near, own_grads, lead_grads = attend(
        "near", 0, scalars, rows, (pk, pv), leads, (own_grads, lead_grads)
    )
    back = [swap(x, QUAD + n) if n < 3 else x for n, x in enumerate(back)]
    quads = [list(range(n, n + QUAD)) for n in range(0, PARTS, QUAD)]
    back_near = lax.all_to_all(
        back_near, "mp", split_axis=0, concat_axis=0, axis_index_groups=quads, tiled=True
    )

    lead_grads, *back[:2] = lax.optimization_barrier((lead_grads, *back[:2]))
    near_grads = send(lead_grads, (1, 0), (3, 2))
    near_sum = (lead_grads + near_grads).astype(BF16)
    near_sum, back[3] = lax.optimization_barrier((near_sum, back[3]))
    back[3] = swap(back[3], QUAD + 3)
    far_grads = send(near_sum, (2, 0))
    near_sum, near_grads = lax.optimization_barrier((near_sum, near_grads))
    base = own_grads + jnp.where(leader, lead_grads + near_grads, 0.0)
    d_keys, d_values = (
        (base[n] + far_grads[n].astype(F32)).astype(BF16)[None] for n in range(2)
    )
    outs = unpack(ids, *back, back_near, base)
    return (*outs, d_keys, d_values)


def solution(mesh):
    rows = P(("dp", "mp"), None)
    heads = P("dp", None, "mp")
    return jax.shard_map(
        local,
        mesh=mesh,
        in_specs=(rows, rows, rows, heads, heads, P("dp"), P("dp"), rows),
        out_specs=(rows, rows, rows, rows, heads, heads),
        check_vma=False,
    )
```
